256 devices in a mesh: dp: 32 (over z_hi, y, core), seq: 8 (over z_lo, x).
Axes of the slice: x: 4, y: 4, z: 8 (z_hi: 4, z_lo: 2; z = z_hi * 2 + z_lo), core: 2. Of those that a mesh axis runs over, the one named last changes fastest.
Arguments:
- layer_input: bfloat16 [32768, 4096], P(('dp', 'seq')), may hold values from -24 to 24
- queries: bfloat16 [32768, 2048], P(('dp', 'seq')), may hold values from -24 to 24
- key_rows: bfloat16 [32768, 2048], P(('dp', 'seq')), may hold values from -24 to 24
- value_rows: bfloat16 [32768, 2048], P(('dp', 'seq')), may hold values from -6 to 6
- output_grad: bfloat16 [32768, 4096], P(('dp', 'seq')), may hold values from -24 to 24
- out_weight: bfloat16 [2048, 4096], P('seq', 'dp'), may hold values from -0.125 to 0.125
- segment_ids: int32 [32, 1024], P('dp', 'seq'), may hold values from 0 to 3, never falling along the last dimension, each value on 1 to 512 neighbouring positions
- timesteps: int32 [32], P('dp'), may hold values from 125 to 1000
- masked_tokens: int32 [32768], P(('dp', 'seq')), may hold values 0 or 1
Outputs:
- grad_query: float32 [4096, 2048], P('dp', 'seq')
- grad_key: float32 [4096, 2048], P('dp', 'seq')
- grad_value: float32 [4096, 2048], P('dp', 'seq')
- grad_out: float32 [2048, 4096], P('seq', 'dp')
The draws below stay inside these ranges and needn't reach their ends.
All inputs are finite; a program needn't handle non-finite values. No bound on the sum of `masked_tokens` on one device may be relied on, other than what follows from the above.
Results may differ from the reference program's by a relative error of at most 0.024.
Values may be sent and summed in bfloat16 or wider, within the bound.
No kernel may reach another device: no remote copies, remote signals or barrier semaphores. Data moves between devices by JAX's collectives and lax.ppermute only.
A program may use at most 128 MiB of HBM per device.

```python
import math
import jax
import jax.numpy as jnp
import numpy as np
from jax import lax

D = 4096
HEADS = 16
HEAD = 128
TOK_DEV = 128
DOCS = 4
TSTEPS = 1000
HD = 2048
LENGTH = 1024
SLABS = 32
TOKENS = 32768
N_DP = 32
N_SEQ = 8


def draw_queries(key, part):
    key = jax.random.fold_in(key, 11)
    values = jax.random.truncated_normal(key, -6.0, 6.0, (TOKENS, HEADS * HEAD), jnp.float32)
    return values.astype(jnp.bfloat16)


def draw_key_rows(key, part):
    key = jax.random.fold_in(key, 23)
    values = jax.random.truncated_normal(key, -6.0, 6.0, (TOKENS, HEADS * HEAD), jnp.float32)
    return values.astype(jnp.bfloat16)


def touch_ends(values, key, smallest, top_value):
    longest = values.shape.index(max(values.shape))
    spots = []
    for shift in (0, 1):
        where = [jax.random.randint(jax.random.fold_in(key, axis), (), 0, length) for axis, length in enumerate(values.shape)]
        where[longest] = (where[longest] + shift) % values.shape[longest]
        spots.append(tuple(where))
    return values.at[spots[0]].set(smallest).at[spots[1]].set(top_value)


def raised(array, key, source, target, parts, factor):
    owner, partner = [(jnp.arange(array.shape[dim]) // (array.shape[dim] // parts)).reshape([-1 if axis == dim else 1 for axis in range(array.ndim)]) for dim in (source, target)]
    chosen = jax.random.permutation(key, parts)[partner]
    strong = (owner == chosen) | (owner == (partner + parts // 2) % parts)
    return jnp.where(strong, factor * array, array)


def level_of(key, shape, shards, low, largest):
    def one(dim, shards_of):
        draws = jax.random.uniform(jax.random.fold_in(jax.random.fold_in(key, 6), dim), (shards_of,), jnp.float32, low / len(shards), largest / len(shards))
        return jnp.repeat(jnp.exp(draws), shape[dim] // shards_of).reshape((-1,) + (1,) * (len(shape) - dim - 1))

    gain = one(*shards[0])
    for cut in shards[1:]:
        gain = gain * one(*cut)
    return gain


def split_up(count, total, bound, slope):
    portions = [(1 << 20) // math.isqrt(grade ** slope) + 1 for grade in range(2, count + 1)]
    rest, holding = total - bound - (count - 1), [1] * (count - 1)
    while rest > 0:
        movable = [i for i in range(count - 1) if holding[i] < bound]
        whole, budget = sum([portions[i] for i in movable]), rest
        for i in movable:
            more = min(bound - holding[i], max(1, budget * portions[i] // whole), rest)
            holding[i] = holding[i] + more
            rest = rest - more
    return np.array([bound] + holding)


def ragged(rng, count, total, reach, lean):
    if count == 2:
        one = jax.random.randint(rng, (), max(1, total - reach), min(reach, total - 1) + 1)
        return jnp.stack([one, total - one])
    sizes = jnp.asarray(split_up(count, total, reach, lean), jnp.int32)
    couples = (count - 1) // 2
    giver, sink = sizes[1:1 + 2 * couples:2], sizes[2:2 + 2 * couples:2]
    slack = jnp.minimum(giver - 1, reach - sink)
    moved = jax.random.randint(jax.random.fold_in(rng, 1), (couples,), 0, 1 << 20) % (slack + 1)
    sizes = sizes.at[1:1 + 2 * couples:2].set(giver - moved).at[2:2 + 2 * couples:2].set(sink + moved)
    return sizes[jax.random.permutation(jax.random.fold_in(rng, 2), count)]


def noise(stream_key, dims, scale, most, shards=(), dtype=jnp.bfloat16):
    values = jax.random.normal(stream_key, dims, jnp.float32) * scale
    if len(shards) > 0:
        values = level_of(stream_key, dims, shards, -0.22, 0.18) * values
    return jnp.clip(values, min=-most, max=most).astype(dtype)


def gaussian_with(rng, extent, scale, most, pieces, heavy, kind=jnp.bfloat16):
    array = scale * jax.random.normal(rng, extent, jnp.float32)
    if pieces:
        array = array * level_of(rng, extent, pieces, -0.22, 0.18)
    return jnp.clip(raised(array, jax.random.fold_in(rng, 3), *heavy), -most, most).astype(kind)


def setup_inputs(seed: int = 0) -> dict:
    key_list = jax.random.split(jax.random.key(seed), 10)
    layer_input = gaussian_with(key_list[0], (TOKENS, D), 1.0, 24.0, ((0, 256),), (0, 1, 256, 6.0))
    queries = draw_queries(jax.random.fold_in(key_list[9], 71), 0)
    key_rows = draw_key_rows(jax.random.fold_in(key_list[9], 71), 0)
    value_rows = noise(key_list[3], (TOKENS, HD), 1.0, 6.0, ((0, 256),))
    output_grad = gaussian_with(key_list[4], (TOKENS, D), 1.0, 24.0, ((0, 256),), (0, 1, 256, 6.0))
    out_weight = noise(key_list[5], (HD, D), HD ** -0.5, 0.125, ((0, 8), (1, 32)))
    segment_ids = jax.vmap(lambda own: jnp.searchsorted(jnp.cumsum(ragged(own, DOCS, LENGTH, LENGTH // 2, 1)), jnp.arange(LENGTH), side="right"))(jax.random.split(key_list[6], SLABS)).reshape((SLABS, LENGTH)).astype(jnp.int32)
    timesteps = touch_ends(jax.random.randint(key_list[7], (SLABS,), TSTEPS // 8, TSTEPS + 1), jax.random.fold_in(key_list[7], 1), TSTEPS // 8, TSTEPS).astype(jnp.int32)
    masked_tokens = touch_ends((jax.random.randint(key_list[8], (TOKENS,), 0, 2) < 1).astype(jnp.int32), jax.random.fold_in(key_list[8], 1), 0, 1)
    return dict(layer_input=layer_input, queries=queries, key_rows=key_rows, value_rows=value_rows, output_grad=output_grad, out_weight=out_weight, segment_ids=segment_ids, timesteps=timesteps, masked_tokens=masked_tokens)


def head_grads(head_query, head_key, head_value, head_dout, same_doc):
    factor = HEAD ** -0.5
    scores = jnp.dot(head_query, head_key.T, preferred_element_type=jnp.float32) * factor
    scores = jnp.where(same_doc, scores, -jnp.inf)
    row_max = jnp.max(scores, axis=-1, keepdims=True)
    shifted = jnp.exp(scores - row_max)
    probs = shifted / jnp.sum(shifted, axis=-1, keepdims=True)
    probs_low = probs.astype(jnp.bfloat16)
    attended = jnp.dot(probs_low, head_value, preferred_element_type=jnp.float32).astype(jnp.bfloat16)
    dprobs = jnp.dot(head_dout, head_value.T, preferred_element_type=jnp.float32)
    row_delta = jnp.sum(probs * dprobs, axis=-1, keepdims=True)
    dscores = (probs * (dprobs - row_delta) * factor).astype(jnp.bfloat16)
    grad_v = jnp.dot(probs_low.T, head_dout, preferred_element_type=jnp.float32).astype(jnp.bfloat16)
    grad_q = jnp.dot(dscores, head_key, preferred_element_type=jnp.float32).astype(jnp.bfloat16)
    grad_k = jnp.dot(dscores.T, head_query, preferred_element_type=jnp.float32).astype(jnp.bfloat16)
    return attended, grad_q, grad_k, grad_v


def split_heads(matrix):
    count = matrix.shape[1] // HEAD
    return matrix.reshape(matrix.shape[0], count, HEAD).transpose(1, 0, 2)


def join_heads(stacked):
    return stacked.transpose(1, 0, 2).reshape(stacked.shape[1], -1)


def attention_grads(query_cols, key_cols, value_cols, dout_cols, seg_row):
    same_doc = seg_row[:, None] == seg_row[None, :]

    def one_head(operands):
        return head_grads(operands[0], operands[1], operands[2], operands[3], same_doc)

    results = lax.map(one_head, (split_heads(query_cols), split_heads(key_cols), split_heads(value_cols), split_heads(dout_cols)))
    return tuple(join_heads(item) for item in results)


def slab_terms(input_slab, query_slab, key_slab, value_slab, grad_slab, seg_row, out_weight):
    dout = jnp.dot(grad_slab, out_weight.T, preferred_element_type=jnp.float32).astype(jnp.bfloat16)
    attended, grad_q, grad_k, grad_v = attention_grads(query_slab, key_slab, value_slab, dout, seg_row)
    term_out = jnp.dot(attended.T, grad_slab, preferred_element_type=jnp.float32).astype(jnp.bfloat16)
    term_q = jnp.dot(input_slab.T, grad_q, preferred_element_type=jnp.float32).astype(jnp.bfloat16)
    term_k = jnp.dot(input_slab.T, grad_k, preferred_element_type=jnp.float32).astype(jnp.bfloat16)
    term_v = jnp.dot(input_slab.T, grad_v, preferred_element_type=jnp.float32).astype(jnp.bfloat16)
    return term_q, term_k, term_v, term_out


def reference(layer_input, queries, key_rows, value_rows, output_grad, out_weight, segment_ids, timesteps, masked_tokens):
    length = TOK_DEV * N_SEQ
    slab_count = N_DP
    width = queries.shape[1]
    model_width = layer_input.shape[1]
    norm_scale = float(layer_input.shape[0]) ** -0.5
    slab_steps = jnp.repeat(timesteps, length).astype(jnp.float32)
    row_weight = masked_tokens.astype(jnp.float32) * (TSTEPS / slab_steps) * norm_scale
    scaled = (output_grad * row_weight[:, None]).astype(jnp.bfloat16)
    stacked_in = (
        layer_input.reshape(slab_count, length, model_width),
        queries.reshape(slab_count, length, width),
        key_rows.reshape(slab_count, length, width),
        value_rows.reshape(slab_count, length, width),
        scaled.reshape(slab_count, length, model_width),
        segment_ids,
    )

    def step(carry, operands):
        terms = slab_terms(operands[0], operands[1], operands[2], operands[3], operands[4], operands[5], out_weight)
        return tuple(total + term.astype(jnp.float32) for total, term in zip(carry, terms)), None

    init = (
        jnp.zeros((model_width, width), jnp.float32),
        jnp.zeros((model_width, width), jnp.float32),
        jnp.zeros((model_width, width), jnp.float32),
        jnp.zeros((width, model_width), jnp.float32),
    )
    totals, unused = lax.scan(step, init, stacked_in)
    return (totals[0], totals[1], totals[2], totals[3])
```

```python
import functools

import jax
import jax.numpy as jnp
from jax import lax
from jax.experimental import pallas as pl
from jax.experimental.pallas import tpu as pltpu
from jax.sharding import Mesh, PartitionSpec as P

HEAD = 128
TSTEPS = 1000
TOK = 128
AXES = ("h", "y", "c", "l", "x")
SIZES = (4, 4, 2, 2, 4)
DP = ("h", "y", "c")
SEQ = ("l", "x")
RELATIVE = [(dl, dx) for dl in range(2) for dx in range(4)]
F32, BF16 = jnp.float32, jnp.bfloat16


def recv(block, axis, offset):
    n = SIZES[AXES.index(axis)]
    return lax.ppermute(block, axis, [((i + offset) % n, i) for i in range(n)])


def gather_z_first(block):
    pair = jnp.concatenate([block, recv(block, "l", 1)], axis=0)
    ring = [pair] + [recv(pair, "x", d) for d in (1, 2, 3)]
    return jnp.concatenate([r[:TOK] for r in ring] + [r[TOK:] for r in ring], axis=0)


def gather_x_first(block):
    ring = [block] + [recv(block, "x", d) for d in (1, 2, 3)]
    return jnp.concatenate(ring + [recv(r, "l", 1) for r in ring], axis=0)


def dot(a, b, dims):
    return lax.dot_general(a, b, (dims, ((), ())), preferred_element_type=F32)


def params(**kw):
    return pltpu.CompilerParams(vmem_limit_bytes=40 * 2**20, **kw)


def reorder_kernel(order_ref, x_ref, dep_ref, o_ref):
    for j in range(o_ref.shape[1] // 128):
        start = pl.multiple_of(order_ref[j] * 128, 128)
        o_ref[:, j * 128 : (j + 1) * 128] = x_ref[:, pl.ds(start, 128)]


def reorder(x, order, dep):
    n = order.shape[0]
    return pl.pallas_call(
        reorder_kernel,
        out_shape=jax.ShapeDtypeStruct((x.shape[0], n * 128), x.dtype),
        in_specs=[
            pl.BlockSpec(memory_space=pltpu.SMEM),
            pl.BlockSpec(memory_space=pltpu.VMEM),
            pl.BlockSpec(memory_space=pl.ANY),
        ],
        out_specs=pl.BlockSpec(memory_space=pltpu.VMEM),
        compiler_params=params(),
        cost_estimate=pl.CostEstimate(flops=0, bytes_accessed=4 * 128 * n * 128, transcendentals=0),
        name="reorder",
    )(order, x, dep)


def load_rows(x_ref, idx_ref, part):
    cols = slice(part * HEAD, (part + 1) * HEAD)
    return jnp.concatenate([x_ref[idx_ref[r], :TOK, cols] for r in range(8)], axis=0)


def forward_kernel(idx_ref, x_ref, att_ref, p_ref):
    factor = HEAD ** (-0.5)
    keys = load_rows(x_ref, idx_ref, 1)
    values = load_rows(x_ref, idx_ref, 2)
    segs = [x_ref[idx_ref[r], TOK : TOK + 16, :HEAD].astype(F32)[:1] for r in range(8)]
    seg_row = jnp.concatenate(segs, axis=1)
    for blk in range(8):
        rows = slice(blk * TOK, (blk + 1) * TOK)
        q = x_ref[idx_ref[blk], :TOK, :HEAD]
        seg_col = jnp.broadcast_to(segs[blk], (TOK, TOK)).T[:, :1]
        scores = dot(q, keys, ((1,), (1,))) * factor
        scores = jnp.where(seg_col == seg_row, scores, -jnp.inf)
        shifted = jnp.exp(scores - jnp.max(scores, axis=-1, keepdims=True))
        probs = shifted * (1.0 / jnp.sum(shifted, axis=-1, keepdims=True))
        low = probs.astype(BF16)
        p_ref[0, rows, :] = low
        att_ref[rows, :] = dot(low, values, ((1,), (0,))).astype(BF16)


def forward(packed, idx):
    return pl.pallas_call(
        forward_kernel,
        grid=(2,),
        out_shape=(
            jax.ShapeDtypeStruct((1024, 256), BF16),
            jax.ShapeDtypeStruct((2, 1024, 1024), BF16),
        ),
        in_specs=[
            pl.BlockSpec(memory_space=pltpu.SMEM),
            pl.BlockSpec((8, TOK + 16, 384), lambda i: (0, 0, i)),
        ],
        out_specs=(
            pl.BlockSpec((1024, HEAD), lambda i: (0, i)),
            pl.BlockSpec((1, 1024, 1024), lambda i: (i, 0, 0)),
        ),
        compiler_params=params(),
        cost_estimate=pl.CostEstimate(
            flops=2 * 2 * 2 * 1024 * 1024 * 128, bytes_accessed=6 * 2**20, transcendentals=2 * 2**20
        ),
        name="attention_forward",
    )(idx, packed)


def backward_kernel(idx_ref, x_ref, p_ref, dout_ref, o_ref, dk_ref, dv_ref):
    factor = HEAD ** (-0.5)
    keys = load_rows(x_ref, idx_ref, 1)
    values = load_rows(x_ref, idx_ref, 2)
    for blk in range(4):
        rows = slice(blk * 256, (blk + 1) * 256)
        q = jnp.concatenate([x_ref[idx_ref[2 * blk + j], :TOK, :HEAD] for j in range(2)], axis=0)
        low = p_ref[0, rows, :]
        dout = dout_ref[rows, :]
        dprobs = dot(dout, values, ((1,), (1,)))
        probs = low.astype(F32)
        delta = jnp.sum(probs * dprobs, axis=-1, keepdims=True)
        dscores = (probs * (dprobs - delta) * factor).astype(BF16)
        o_ref[rows, :HEAD] = dot(dscores, keys, ((1,), (0,))).astype(BF16)
        dk = dot(dscores, q, ((0,), (0,)))
        dv = dot(low, dout, ((0,), (0,)))
        if blk == 0:
            dk_ref[...] = dk
            dv_ref[...] = dv
        else:
            dk_ref[...] += dk
            dv_ref[...] += dv
    o_ref[:, HEAD : 2 * HEAD] = dk_ref[...].astype(BF16)
    o_ref[:, 2 * HEAD :] = dv_ref[...].astype(BF16)


def backward(packed, idx, probs, dout):
    return pl.pallas_call(
        backward_kernel,
        grid=(2,),
        out_shape=jax.ShapeDtypeStruct((1024, 768), BF16),
        in_specs=[
            pl.BlockSpec(memory_space=pltpu.SMEM),
            pl.BlockSpec((8, TOK + 16, 384), lambda i: (0, 0, i)),
            pl.BlockSpec((1, 1024, 1024), lambda i: (i, 0, 0)),
            pl.BlockSpec((1024, HEAD), lambda i: (0, i)),
        ],
        out_specs=pl.BlockSpec((1024, 384), lambda i: (0, i)),
        scratch_shapes=[pltpu.VMEM((1024, HEAD), F32), pltpu.VMEM((1024, HEAD), F32)],
        compiler_params=params(),
        cost_estimate=pl.CostEstimate(
            flops=4 * 2 * 2 * 1024 * 1024 * 128, bytes_accessed=8 * 2**20, transcendentals=0
        ),
        name="attention_backward",
    )(idx, packed, probs, dout)


def sum_over_y(mine, pick):
    total = pick(0).astype(F32)
    for dy in (1, 2, 3):
        total = total + recv(pick(dy), "y", 4 - dy).astype(F32)
    return total


def shards(
    layer_input,
    queries,
    key_rows,
    value_rows,
    output_grad,
    out_weight,
    segment_ids,
    timesteps,
    masked_tokens,
):
    total_tokens = layer_input.shape[0] * 256
    norm_scale = float(total_tokens) ** (-0.5)
    h, y, c, l, x = (lax.axis_index(a) for a in AXES)
    idx = jnp.stack([((l + dl) % 2) * 4 + (x + dx) % 4 for dl, dx in RELATIVE]).astype(jnp.int32)

    out_rows = lax.all_gather(out_weight, DP, axis=1, tiled=True)

    stacked = jnp.stack([m.reshape(TOK, 8, 2, HEAD) for m in (queries, key_rows, value_rows)], axis=3)
    body = stacked.reshape(TOK, 8, 768).transpose(1, 0, 2)
    segs = jnp.broadcast_to(jnp.tile(segment_ids[0].astype(BF16), 6), (8, 16, 768))
    packed = lax.all_to_all(
        jnp.concatenate([body, segs], axis=1), SEQ, split_axis=0, concat_axis=0, tiled=True
    )

    row_weight = masked_tokens.astype(F32) * (TSTEPS / timesteps.astype(F32)) * norm_scale
    scaled = (output_grad * row_weight[:, None]).astype(BF16)
    half = scaled.shape[1] // 2
    scaled_a = gather_z_first(scaled[:, :half])
    scaled_b = gather_x_first(scaled[:, half:])

    attended, probs = forward(packed, idx)
    dout = (
        dot(scaled_a, out_rows[:, :half], ((1,), (1,)))
        + dot(scaled_b, out_rows[:, half:], ((1,), (1,)))
    ).astype(BF16)
    dqkv = backward(packed, idx, probs, dout)

    terms = [dot(s, attended, ((0,), (0,))).astype(BF16) for s in (scaled_a, scaled_b)]
    terms = jnp.stack([t.reshape(2, 4, 2, 128, 256) for t in terms]).reshape(4, 4, 2, 128, 256)
    pick_c = lambda i: lax.dynamic_index_in_dim(terms, i, 2, keepdims=False)
    mine = (pick_c(c).astype(F32) + recv(pick_c(1 - c), "c", 1).astype(F32)).astype(BF16)
    mine = sum_over_y(
        mine, lambda dy: lax.dynamic_index_in_dim(mine, (y + dy) % 4, 1, keepdims=False)
    ).astype(BF16)
    pick_h = lambda dh: lax.dynamic_index_in_dim(mine, (h + dh) % 4, 0, keepdims=False)
    grad_out = pick_h(0).astype(F32)
    for dh in (1, 2, 3):
        grad_out = grad_out + recv(pick_h(dh), "h", 4 - dh).astype(F32)

    grads = 0.0
    dep = scaled_a
    for i, dh in enumerate((2, 1, 3, 0)):
        order = jnp.stack(
            [
                ((h + dh) % 4) * 8 + ((y + dy) % 4) * 2 + (c + dc) % 2
                for dc in (1, 0)
                for dy in range(4)
            ]
        ).astype(jnp.int32)
        columns = reorder(layer_input, order, dep)
        slab = (gather_x_first if i % 2 == 0 else gather_z_first)(columns)
        if i % 2 == 1:
            dep = slab
        term = dot(slab, dqkv, ((0,), (0,))).astype(BF16).reshape(2, 4, 128, 768)
        mine_i = (term[1].astype(F32) + recv(term[0], "c", 1).astype(F32)).astype(BF16)
        part = sum_over_y(mine_i, lambda dy: mine_i[dy])
        if dh:
            part = recv(part.astype(BF16), "h", 4 - dh).astype(F32)
        grads = grads + part
    grads = grads.reshape(128, 2, 3, HEAD)
    grad_q, grad_k, grad_v = (grads[:, :, j].reshape(128, 256) for j in range(3))
    return grad_q, grad_k, grad_v, grad_out.T


def solution(mesh):
    view = Mesh(mesh.devices.reshape(SIZES), AXES)
    tokens = P(DP + SEQ, None)
    return jax.shard_map(
        shards,
        mesh=view,
        in_specs=(
            tokens,
            tokens,
            tokens,
            tokens,
            tokens,
            P(SEQ, DP),
            P(DP, SEQ),
            P(DP),
            P(DP + SEQ),
        ),
        out_specs=(P(DP, SEQ), P(DP, SEQ), P(DP, SEQ), P(SEQ, DP)),
        check_vma=False,
    )
```

```python
import jax
import jax.numpy as jnp
from jax import lax
from jax.experimental import pallas as pl
from jax.experimental.pallas import tpu as pltpu
from jax.sharding import Mesh, PartitionSpec as P

HEAD = 128
TSTEPS = 1000
TOK = 128
AXES = ("h", "y", "c", "l", "x")
SIZES = (4, 4, 2, 2, 4)
DP = ("h", "y", "c")
SEQ = ("l", "x")
RELATIVE = [(dl, dx) for dl in range(2) for dx in range(4)]
HALF = 2048
F32, BF16 = jnp.float32, jnp.bfloat16
VMEM = pl.BlockSpec(memory_space=pltpu.VMEM)
SMEM = pl.BlockSpec(memory_space=pltpu.SMEM)
HBM = pl.BlockSpec(memory_space=pltpu.HBM)


def recv(block, axis, offset):
    n = SIZES[AXES.index(axis)]
    return lax.ppermute(block, axis, [((i + offset) % n, i) for i in range(n)])


def send_zz(block, target, only=None):
    pairs = []
    for h in range(4):
        for l in range(2):
            if only is None or only == h // 2:
                h1, h0, to_l = target(h // 2, h % 2, l)
                pairs.append((h * 2 + l, (h1 * 2 + h0) * 2 + to_l))
    return lax.ppermute(block, ("h", "l"), pairs)


def ring(block):
    near, far, across = recv(block, "x", 1), recv(block, "x", 3), recv(block, "x", 2)
    return [block, near, across, far]


def dot(a, b, dims):
    return lax.dot_general(a, b, (dims, ((), ())), preferred_element_type=F32)


def call(kernel, name, inputs, specs, out_shape, out_specs, deps=(), grid=(1,), scratch=()):
    n, m = len(inputs), len(deps)

    def body(*refs):
        kernel(*refs[:n], *refs[n + m :])

    def whole(spec, array):
        zeros = (0,) * len(array.shape)
        return pl.BlockSpec(array.shape, lambda i: zeros) if spec is VMEM else spec

    outs = out_shape if isinstance(out_shape, tuple) else (out_shape,)
    out_specs = out_specs if isinstance(out_specs, tuple) else (out_specs,)
    results = pl.pallas_call(
        body,
        grid=grid,
        out_shape=outs,
        in_specs=[whole(s, a) for s, a in zip(specs, inputs)] + [HBM] * m,
        out_specs=tuple(whole(s, a) for s, a in zip(out_specs, outs)),
        scratch_shapes=scratch,
        compiler_params=pltpu.CompilerParams(vmem_limit_bytes=60 * 2**20),
        cost_estimate=pl.CostEstimate(flops=0, bytes_accessed=0, transcendentals=0),
        name=name,
    )(*inputs, *deps)
    return results if isinstance(out_shape, tuple) else results[0]


def gate(x, deps):
    return pl.pallas_call(
        lambda *refs: None,
        out_shape=jax.ShapeDtypeStruct(x.shape, x.dtype),
        in_specs=[HBM] * (1 + len(deps)),
        out_specs=HBM,
        input_output_aliases={0: 0},
        cost_estimate=pl.CostEstimate(flops=0, bytes_accessed=0, transcendentals=0),
        name="gate",
    )(x, *deps)


def shape(*dims, dtype=BF16):
    return jax.ShapeDtypeStruct(dims, dtype)


def scale_kernel(place_ref, g_ref, w_ref, keep_ref, send_ref):
    w = w_ref[...]
    mine = pl.multiple_of(place_ref[3] * HALF, HALF)
    other = pl.multiple_of((1 - place_ref[3]) * HALF, HALF)
    keep_ref[...] = (g_ref[:, pl.ds(mine, HALF)].astype(F32) * w).astype(BF16)
    send_ref[...] = (g_ref[:, pl.ds(other, HALF)].astype(F32) * w).astype(BF16)


def pack_kernel(q_ref, k_ref, v_ref, s_ref, o_ref):
    segs = jnp.broadcast_to(s_ref[...].astype(F32), (16, TOK)).astype(BF16)
    for dest in range(8):
        for head in range(2):
            cols = slice((dest * 2 + head) * HEAD, (dest * 2 + head + 1) * HEAD)
            for j, ref in enumerate((q_ref, k_ref, v_ref)):
                at = slice((head * 3 + j) * HEAD, (head * 3 + j + 1) * HEAD)
                o_ref[dest, :TOK, at] = ref[:, cols]
                o_ref[dest, TOK:, at] = segs


def reorder_kernel(order_ref, x_ref, *o_refs):
    for i, ref in enumerate(o_refs):
        for j in range(16):
            start = pl.multiple_of(order_ref[i * 16 + j] * 128, 128)
            ref[:, j * 128 : (j + 1) * 128] = x_ref[:, pl.ds(start, 128)]


def pair_kernel(a_ref, b_ref, o_ref):
    o_ref[:TOK] = a_ref[...]
    o_ref[TOK:] = b_ref[...]


def load_rows(x_ref, idx_ref, part):
    cols = slice(part * HEAD, (part + 1) * HEAD)
    return jnp.concatenate([x_ref[idx_ref[r], :TOK, cols] for r in range(8)], axis=0)


def forward_kernel(idx_ref, x_ref, att_ref, p_ref):
    factor = HEAD ** (-0.5)
    keys = load_rows(x_ref, idx_ref, 1)
    values = load_rows(x_ref, idx_ref, 2)
    segs = [x_ref[idx_ref[r], TOK : TOK + 16, :HEAD].astype(F32)[:1] for r in range(8)]
    seg_row = jnp.concatenate(segs, axis=1)
    for blk in range(8):
        rows = slice(blk * TOK, (blk + 1) * TOK)
        q = x_ref[idx_ref[blk], :TOK, :HEAD]
        seg_col = jnp.broadcast_to(segs[blk], (TOK, TOK)).T[:, :1]
        scores = dot(q, keys, ((1,), (1,))) * factor
        scores = jnp.where(seg_col == seg_row, scores, -jnp.inf)
        shifted = jnp.exp(scores - jnp.max(scores, axis=-1, keepdims=True))
        probs = shifted * (1.0 / jnp.sum(shifted, axis=-1, keepdims=True))
        low = probs.astype(BF16)
        p_ref[0, rows, :] = low
        att_ref[:, rows] = dot(low, values, ((1,), (0,))).T.astype(BF16)


def backward_kernel(idx_ref, x_ref, p_ref, dout_ref, o_ref, dk_ref, dv_ref):
    factor = HEAD ** (-0.5)
    keys = load_rows(x_ref, idx_ref, 1)
    values = load_rows(x_ref, idx_ref, 2)
    for blk in range(4):
        rows = slice(blk * 256, (blk + 1) * 256)
        q = jnp.concatenate([x_ref[idx_ref[2 * blk + j], :TOK, :HEAD] for j in range(2)], axis=0)
        low = p_ref[0, rows, :]
        dout = dout_ref[rows, :]
        dprobs = dot(dout, values, ((1,), (1,)))
        probs = low.astype(F32)
        delta = jnp.sum(probs * dprobs, axis=-1, keepdims=True)
        dscores = (probs * (dprobs - delta) * factor).astype(BF16)
        o_ref[:HEAD, rows] = dot(dscores, keys, ((1,), (0,))).T.astype(BF16)
        dk = dot(q, dscores, ((0,), (0,)))
        dv = dot(dout, low, ((0,), (0,)))
        if blk == 0:
            dk_ref[...] = dk
            dv_ref[...] = dv
        else:
            dk_ref[...] += dk
            dv_ref[...] += dv
    o_ref[HEAD : 2 * HEAD, :] = dk_ref[...].astype(BF16)
    o_ref[2 * HEAD :, :] = dv_ref[...].astype(BF16)


def flipped(lhs):
    return jnp.concatenate([lhs[:, 512:], lhs[:, :512]], axis=1)


def by_x(lhs_ref, x, flip):
    blocks = []
    for at_x in range(4):
        for dl in range(2):
            row = (1 - dl if flip else dl) * 4 + (at_x - x + 4) % 4
            blocks.append(lhs_ref[:, pl.ds(pl.multiple_of(row * TOK, TOK), TOK)])
    return jnp.concatenate(blocks, axis=1)


def dout_kernel(*refs):
    pieces, (w_ref, place_ref, keep_ref, send_ref) = refs[:8], refs[8:]
    mine = pl.multiple_of(place_ref[3] * HALF, HALF)
    other = pl.multiple_of((1 - place_ref[3]) * HALF, HALF)
    for quarter in range(4):
        left = jnp.concatenate([p[...] for p in pieces[2 * quarter : 2 * quarter + 2]], axis=0)
        rows = slice(quarter * 256, (quarter + 1) * 256)
        keep_ref[rows, :] = dot(left, w_ref[:, pl.ds(mine, HALF)], ((1,), (1,)))
        at = (quarter + 2) % 4 * 256
        total = dot(left, w_ref[:, pl.ds(other, HALF)], ((1,), (1,)))
        send_ref[at : at + 256, :] = total.astype(BF16)


def out_terms_kernel(*refs):
    pieces, (own_ref, other_ref, place_ref, send_ref, keep_ref) = refs[:8], refs[8:]
    h0, c = place_ref[0] % 2, place_ref[2]
    att = jnp.concatenate([own_ref[...], flipped(other_ref[...])], axis=0)
    for tile in range(8):
        cols = slice(tile * 256, (tile + 1) * 256)
        rhs = jnp.concatenate([p[:, cols] for p in pieces], axis=0)
        term = dot(att, rhs, ((1,), (0,))).astype(BF16)
        at = tile % 4
        a = (tile // 4 + h0) % 2
        send_ref[at, a] = jnp.where(c == 0, term[:, 128:], term[:, :128])
        keep_ref[at, a] = jnp.where(c == 0, term[:, :128], term[:, 128:])


def term_blocks(lhs, slab, place, flip, deps):
    n, m = len(lhs), sum(a.shape[0] for a in lhs)

    def kernel(*refs):
        slab_ref, place_ref, send_ref, keep_ref = refs[n:]
        left = jnp.concatenate([by_x(r, place_ref[4], flip) for r in refs[:n]], axis=0)
        for tile in range(8):
            cols = slice(tile * 256, (tile + 1) * 256)
            term = dot(left, slab_ref[:, cols], ((1,), (0,))).astype(BF16)
            out = send_ref if tile % 4 < 2 else keep_ref
            out[(tile % 2) * 2, tile // 4] = term[:, :128]
            out[(tile % 2) * 2 + 1, tile // 4] = term[:, 128:]

    return call(
        kernel,
        "term_blocks",
        list(lhs) + [slab, place],
        [VMEM] * (n + 1) + [SMEM],
        (shape(4, 2, m, 128), shape(4, 2, m, 128)),
        (VMEM, VMEM),
        deps=deps,
    )


def finish_kernel(*refs):
    for head in range(2):
        for j in range(3):
            rows = slice((head * 3 + j) * HEAD, (head * 3 + j + 1) * HEAD)
            total = sum(r[rows, :].astype(F32) for r in refs[:8])
            refs[8 + j][:, head * HEAD : (head + 1) * HEAD] = total.T


def add_low(a, b):
    return (a.astype(F32) + b.astype(F32)).astype(BF16)


def shards(
    layer_input,
    queries,
    key_rows,
    value_rows,
    output_grad,
    out_weight,
    segment_ids,
    timesteps,
    masked_tokens,
):
    total_tokens = layer_input.shape[0] * 256
    norm_scale = float(total_tokens) ** (-0.5)
    h, y, c, l, x = (lax.axis_index(a) for a in AXES)
    idx = jnp.stack([((l + dl) % 2) * 4 + (x + dx) % 4 for dl, dx in RELATIVE]).astype(jnp.int32)
    place = jnp.stack([h, y, c, l, x]).astype(jnp.int32)

    out_rows = send_zz(out_weight, lambda h1, h0, to_l: (to_l, h0, h1))
    out_rows = lax.all_gather(out_rows, DP, axis=1, tiled=True)

    row_weight = masked_tokens.astype(F32) * (TSTEPS / timesteps.astype(F32)) * norm_scale
    scaled_keep, scaled_send = call(
        scale_kernel,
        "scale",
        [place, output_grad, row_weight[:, None]],
        [SMEM, VMEM, VMEM],
        (shape(TOK, HALF), shape(TOK, HALF)),
        (VMEM, VMEM),
    )
    scaled_pair = recv(scaled_send, "l", 1)
    scaled = ring(scaled_keep)
    order = [
        ((half * 2 + (h + a) % 2) * 4 + at_y) * 2 + (c + dc) % 2
        for half in (l, 1 - l)
        for a in (1, 0)
        for dc in (1, 0)
        for at_y in range(4)
    ]
    layer_keep, layer_send = call(
        reorder_kernel,
        "reorder",
        [jnp.stack(order).astype(jnp.int32), layer_input],
        [SMEM, VMEM],
        (shape(TOK, HALF),) * 2,
        (VMEM,) * 2,
        deps=[scaled_keep],
    )
    layer_pair = recv(layer_send, "l", 1)

    to_heads = call(
        pack_kernel,
        "pack",
        [queries, key_rows, value_rows, segment_ids],
        [VMEM] * 4,
        shape(8, TOK + 16, 768),
        VMEM,
        deps=[scaled_keep],
    )
    packed = lax.all_to_all(to_heads, SEQ, split_axis=0, concat_axis=0, tiled=True)
    scaled = scaled + ring(gate(scaled_pair, [packed] + scaled[1:]))

    attended, probs = call(
        forward_kernel,
        "attention_forward",
        [idx, packed],
        [SMEM, pl.BlockSpec((8, TOK + 16, 384), lambda i: (0, 0, i))],
        (shape(256, 1024), shape(2, 1024, 1024)),
        (
            pl.BlockSpec((HEAD, 1024), lambda i: (i, 0)),
            pl.BlockSpec((1, 1024, 1024), lambda i: (i, 0, 0)),
        ),
        grid=(2,),
    )
    attended_pair = recv(attended, "l", 1)
    layer = call(
        pair_kernel,
        "pair",
        [layer_keep, layer_pair],
        [VMEM, VMEM],
        shape(2 * TOK, HALF),
        VMEM,
        deps=[attended] + scaled[5:],
    )
    slab = lax.all_gather(layer, "x", axis=0, tiled=True)
    dout_keep, dout_send = call(
        dout_kernel,
        "dout",
        scaled + [out_rows, place],
        [VMEM] * 9 + [SMEM],
        (shape(1024, 256, dtype=F32), shape(1024, 256)),
        (VMEM, VMEM),
        deps=[layer],
    )
    dout = (dout_keep + recv(dout_send, "l", 1).astype(F32)).astype(BF16)

    out_send, out_keep = call(
        out_terms_kernel,
        "out_terms",
        scaled + [attended, attended_pair, place],
        [VMEM] * 10 + [SMEM],
        (shape(4, 2, 512, 128), shape(4, 2, 512, 128)),
        (VMEM, VMEM),
        deps=[dout_send],
    )

    def backward(head, deps):
        return call(
            backward_kernel,
            "attention_backward",
            [idx, packed, probs, dout],
            [
                SMEM,
                pl.BlockSpec((8, TOK + 16, 384), lambda i: (0, 0, head)),
                pl.BlockSpec((1, 1024, 1024), lambda i: (head, 0, 0)),
                pl.BlockSpec((1024, HEAD), lambda i: (0, head)),
            ],
            shape(384, 1024),
            pl.BlockSpec((384, 1024), lambda i: (0, 0)),
            deps=deps,
            scratch=[pltpu.VMEM((HEAD, 1024), F32), pltpu.VMEM((HEAD, 1024), F32)],
        )

    terms_t = [backward(0, [out_keep])]
    terms_t.append(backward(1, [terms_t[0]]))
    terms_pair = [recv(t, "l", 1) for t in terms_t]

    def core_sum(send, keep):
        return add_low(keep, recv(send, "c", 1))

    def y_sum(blocks):
        arrived = lax.all_to_all(blocks, "y", split_axis=0, concat_axis=0, tiled=True)
        return jnp.sum(arrived.astype(F32), axis=0).astype(BF16)

    out_blocks = core_sum(gate(out_send, [terms_t[1]]), out_keep)
    out_part = y_sum(out_blocks)
    grad_out = 0.0
    for a in range(2):
        for b in range(2):
            chosen = lax.dynamic_slice_in_dim(out_part[a], (h // 2 + b + l) % 2 * 256, 256, 0)
            chosen = send_zz(chosen, lambda h1, h0, l: (l, h0 ^ a, h1 ^ b))
            grad_out = grad_out + chosen.astype(F32)

    deps = [out_part, terms_pair[0]]
    blocks = core_sum(*term_blocks(terms_t, slab, place, False, deps))
    part = y_sum(blocks)
    full = []
    for i, a in enumerate((1, 0)):
        for s in range(2):
            full.append(send_zz(part[i], lambda h1, h0, l: (l, h0 ^ a, l), s))
    blocks = core_sum(*term_blocks(terms_pair, slab, place, True, [part]))
    part = gate(y_sum(blocks), [grad_out] + full)
    for i, a in enumerate((1, 0)):
        for s in range(2):
            full.append(send_zz(part[i], lambda h1, h0, l: (l, h0 ^ a, 1 - l), s))
    grad_q, grad_k, grad_v = call(
        finish_kernel,
        "finish",
        full,
        [VMEM] * 8,
        tuple(shape(128, 256, dtype=F32) for _ in range(3)),
        (VMEM,) * 3,
    )
    return grad_q, grad_k, grad_v, grad_out


def solution(mesh):
    view = Mesh(mesh.devices.reshape(SIZES), AXES)
    tokens = P(DP + SEQ, None)
    return jax.shard_map(
        shards,
        mesh=view,
        in_specs=(
            tokens,
            tokens,
            tokens,
            tokens,
            tokens,
            P(SEQ, DP),
            P(DP, SEQ),
            P(DP),
            P(DP + SEQ),
        ),
        out_specs=(P(DP, SEQ), P(DP, SEQ), P(DP, SEQ), P(SEQ, DP)),
        check_vma=False,
    )
```

```python
import jax
import jax.numpy as jnp
from jax import lax
from jax.experimental import pallas as pl
from jax.experimental.pallas import tpu as pltpu
from jax.sharding import Mesh, PartitionSpec as P

HEAD = 128
TSTEPS = 1000
TOK = 128
AXES = ("h", "y", "c", "l", "x")
SIZES = (4, 4, 2, 2, 4)
DP = ("h", "y", "c")
SEQ = ("l", "x")
RELATIVE = [(dl, dx) for dl in range(2) for dx in range(4)]
HALF = 2048
F32, BF16 = jnp.float32, jnp.bfloat16
VMEM = pl.BlockSpec(memory_space=pltpu.VMEM)
SMEM = pl.BlockSpec(memory_space=pltpu.SMEM)
HBM = pl.BlockSpec(memory_space=pltpu.HBM)


def recv(block, axis, offset):
    n = SIZES[AXES.index(axis)]
    return lax.ppermute(block, axis, [((i + offset) % n, i) for i in range(n)])


def send_zz(block, target, only=None):
    pairs = []
    for h in range(4):
        for l in range(2):
            if only is None or only == h // 2:
                h1, h0, to_l = target(h // 2, h % 2, l)
                pairs.append((h * 2 + l, (h1 * 2 + h0) * 2 + to_l))
    return lax.ppermute(block, ("h", "l"), pairs)


def ring(block):
    near, far, across = recv(block, "x", 1), recv(block, "x", 3), recv(block, "x", 2)
    return [block, near, across, far]


def dot(a, b, dims):
    return lax.dot_general(a, b, (dims, ((), ())), preferred_element_type=F32)


def call(kernel, name, inputs, specs, out_shape, out_specs, deps=(), grid=(1,), scratch=()):
    n, m = len(inputs), len(deps)

    def body(*refs):
        kernel(*refs[:n], *refs[n + m :])

    def whole(spec, array):
        zeros = (0,) * len(array.shape)
        return pl.BlockSpec(array.shape, lambda i: zeros) if spec is VMEM else spec

    outs = out_shape if isinstance(out_shape, tuple) else (out_shape,)
    out_specs = out_specs if isinstance(out_specs, tuple) else (out_specs,)
    results = pl.pallas_call(
        body,
        grid=grid,
        out_shape=outs,
        in_specs=[whole(s, a) for s, a in zip(specs, inputs)] + [HBM] * m,
        out_specs=tuple(whole(s, a) for s, a in zip(out_specs, outs)),
        scratch_shapes=scratch,
        compiler_params=pltpu.CompilerParams(vmem_limit_bytes=60 * 2**20),
        cost_estimate=pl.CostEstimate(flops=0, bytes_accessed=0, transcendentals=0),
        name=name,
    )(*inputs, *deps)
    return results if isinstance(out_shape, tuple) else results[0]


def gate(x, deps):
    return pl.pallas_call(
        lambda *refs: None,
        out_shape=jax.ShapeDtypeStruct(x.shape, x.dtype),
        in_specs=[HBM] * (1 + len(deps)),
        out_specs=HBM,
        input_output_aliases={0: 0},
        cost_estimate=pl.CostEstimate(flops=0, bytes_accessed=0, transcendentals=0),
        name="gate",
    )(x, *deps)


def shape(*dims, dtype=BF16):
    return jax.ShapeDtypeStruct(dims, dtype)


def scale_kernel(place_ref, g_ref, w_ref, keep_ref, send_ref):
    w = w_ref[...]
    mine = pl.multiple_of(place_ref[3] * HALF, HALF)
    other = pl.multiple_of((1 - place_ref[3]) * HALF, HALF)
    keep_ref[...] = (g_ref[:, pl.ds(mine, HALF)].astype(F32) * w).astype(BF16)
    send_ref[...] = (g_ref[:, pl.ds(other, HALF)].astype(F32) * w).astype(BF16)


def pack_kernel(q_ref, k_ref, v_ref, s_ref, o_ref):
    segs = jnp.broadcast_to(s_ref[...].astype(F32), (16, TOK)).astype(BF16)
    for dest in range(8):
        for head in range(2):
            cols = slice((dest * 2 + head) * HEAD, (dest * 2 + head + 1) * HEAD)
            for j, ref in enumerate((q_ref, k_ref, v_ref)):
                at = slice((head * 3 + j) * HEAD, (head * 3 + j + 1) * HEAD)
                o_ref[dest, :TOK, at] = ref[:, cols]
                o_ref[dest, TOK:, at] = segs


def reorder_kernel(order_ref, x_ref, *o_refs):
    for i, ref in enumerate(o_refs):
        for j in range(16):
            start = pl.multiple_of(order_ref[i * 16 + j] * 128, 128)
            ref[:, j * 128 : (j + 1) * 128] = x_ref[:, pl.ds(start, 128)]


def pair_kernel(a_ref, b_ref, o_ref):
    o_ref[:TOK] = a_ref[...]
    o_ref[TOK:] = b_ref[...]


def load_rows(x_ref, idx_ref, part):
    cols = slice(part * HEAD, (part + 1) * HEAD)
    return jnp.concatenate([x_ref[idx_ref[r], :TOK, cols] for r in range(8)], axis=0)


def forward_kernel(idx_ref, x_ref, att_ref, p_ref):
    factor = HEAD ** (-0.5)
    keys = load_rows(x_ref, idx_ref, 1)
    values = load_rows(x_ref, idx_ref, 2)
    segs = [x_ref[idx_ref[r], TOK : TOK + 16, :HEAD].astype(F32)[:1] for r in range(8)]
    seg_row = jnp.concatenate(segs, axis=1)
    for blk in range(8):
        rows = slice(blk * TOK, (blk + 1) * TOK)
        q = x_ref[idx_ref[blk], :TOK, :HEAD]
        seg_col = jnp.broadcast_to(segs[blk], (TOK, TOK)).T[:, :1]
        scores = dot(q, keys, ((1,), (1,))) * factor
        scores = jnp.where(seg_col == seg_row, scores, -jnp.inf)
        shifted = jnp.exp(scores - jnp.max(scores, axis=-1, keepdims=True))
        probs = shifted * (1.0 / jnp.sum(shifted, axis=-1, keepdims=True))
        low = probs.astype(BF16)
        p_ref[0, rows, :] = low
        att_ref[:, rows] = dot(low, values, ((1,), (0,))).T.astype(BF16)


def backward_kernel(idx_ref, x_ref, p_ref, dout_ref, o_ref, dk_ref, dv_ref):
    factor = HEAD ** (-0.5)
    keys = load_rows(x_ref, idx_ref, 1)
    values = load_rows(x_ref, idx_ref, 2)
    for blk in range(4):
        rows = slice(blk * 256, (blk + 1) * 256)
        q = jnp.concatenate([x_ref[idx_ref[2 * blk + j], :TOK, :HEAD] for j in range(2)], axis=0)
        low = p_ref[0, rows, :]
        dout = dout_ref[rows, :]
        dprobs = dot(dout, values, ((1,), (1,)))
        probs = low.astype(F32)
        delta = jnp.sum(probs * dprobs, axis=-1, keepdims=True)
        dscores = (probs * (dprobs - delta) * factor).astype(BF16)
        o_ref[:HEAD, rows] = dot(dscores, keys, ((1,), (0,))).T.astype(BF16)
        dk = dot(q, dscores, ((0,), (0,)))
        dv = dot(dout, low, ((0,), (0,)))
        if blk == 0:
            dk_ref[...] = dk
            dv_ref[...] = dv
        else:
            dk_ref[...] += dk
            dv_ref[...] += dv
    o_ref[HEAD : 2 * HEAD, :] = dk_ref[...].astype(BF16)
    o_ref[2 * HEAD :, :] = dv_ref[...].astype(BF16)


def flipped(lhs):
    return jnp.concatenate([lhs[:, 512:], lhs[:, :512]], axis=1)


def by_x(lhs_ref, x, flip):
    blocks = []
    for at_x in range(4):
        for dl in range(2):
            row = (1 - dl if flip else dl) * 4 + (at_x - x + 4) % 4
            blocks.append(lhs_ref[:, pl.ds(pl.multiple_of(row * TOK, TOK), TOK)])
    return jnp.concatenate(blocks, axis=1)


def dout_kernel(*refs):
    pieces, (w_ref, place_ref, keep_ref, send_ref) = refs[:8], refs[8:]
    mine = pl.multiple_of(place_ref[3] * HALF, HALF)
    other = pl.multiple_of((1 - place_ref[3]) * HALF, HALF)
    for quarter in range(4):
        left = jnp.concatenate([p[...] for p in pieces[2 * quarter : 2 * quarter + 2]], axis=0)
        rows = slice(quarter * 256, (quarter + 1) * 256)
        keep_ref[rows, :] = dot(left, w_ref[:, pl.ds(mine, HALF)], ((1,), (1,)))
        at = (quarter + 2) % 4 * 256
        total = dot(left, w_ref[:, pl.ds(other, HALF)], ((1,), (1,)))
        send_ref[at : at + 256, :] = total.astype(BF16)


def out_terms_kernel(*refs):
    pieces, (own_ref, other_ref, place_ref, send_ref, keep_ref) = refs[:8], refs[8:]
    h0, c = place_ref[0] % 2, place_ref[2]
    att = jnp.concatenate([own_ref[...], flipped(other_ref[...])], axis=0)
    for tile in range(8):
        cols = slice(tile * 256, (tile + 1) * 256)
        rhs = jnp.concatenate([p[:, cols] for p in pieces], axis=0)
        term = dot(att, rhs, ((1,), (0,))).astype(BF16)
        at = tile % 4
        a = (tile // 4 + h0) % 2
        send_ref[at, a] = jnp.where(c == 0, term[:, 128:], term[:, :128])
        keep_ref[at, a] = jnp.where(c == 0, term[:, :128], term[:, 128:])


def term_blocks(lhs, slab, place, flip, deps):
    m = lhs.shape[0]

    def kernel(lhs_ref, slab_ref, place_ref, send_ref, keep_ref):
        left = by_x(lhs_ref, place_ref[4], flip)
        for tile in range(8):
            cols = slice(tile * 256, (tile + 1) * 256)
            term = dot(left, slab_ref[:, cols], ((1,), (0,))).astype(BF16)
            out = send_ref if tile % 4 < 2 else keep_ref
            out[tile % 2 * 2, tile // 4] = term[:, :128]
            out[tile % 2 * 2 + 1, tile // 4] = term[:, 128:]

    return call(
        kernel,
        "term_blocks",
        [lhs, slab, place],
        [VMEM, VMEM, SMEM],
        (shape(4, 2, m, 128), shape(4, 2, m, 128)),
        (VMEM, VMEM),
        deps=deps,
    )


def finish_kernel(*refs):
    for head in range(2):
        for j in range(3):
            rows = slice((head * 3 + j) * HEAD, (head * 3 + j + 1) * HEAD)
            total = sum(r[rows, :].astype(F32) for r in refs[:8])
            refs[8 + j][:, head * HEAD : (head + 1) * HEAD] = total.T


def add_low(a, b):
    return (a.astype(F32) + b.astype(F32)).astype(BF16)


def shards(
    layer_input,
    queries,
    key_rows,
    value_rows,
    output_grad,
    out_weight,
    segment_ids,
    timesteps,
    masked_tokens,
):
    total_tokens = layer_input.shape[0] * 256
    norm_scale = float(total_tokens) ** (-0.5)
    h, y, c, l, x = (lax.axis_index(a) for a in AXES)
    idx = jnp.stack([((l + dl) % 2) * 4 + (x + dx) % 4 for dl, dx in RELATIVE]).astype(jnp.int32)
    place = jnp.stack([h, y, c, l, x]).astype(jnp.int32)

    out_rows = send_zz(out_weight, lambda h1, h0, to_l: (to_l, h0, h1))
    out_rows = lax.all_gather(out_rows, DP, axis=1, tiled=True)

    row_weight = masked_tokens.astype(F32) * (TSTEPS / timesteps.astype(F32)) * norm_scale
    scaled_keep, scaled_send = call(
        scale_kernel,
        "scale",
        [place, output_grad, row_weight[:, None]],
        [SMEM, VMEM, VMEM],
        (shape(TOK, HALF), shape(TOK, HALF)),
        (VMEM, VMEM),
    )
    scaled_pair = recv(scaled_send, "l", 1)
    scaled = ring(scaled_keep)
    order = [
        ((half * 2 + (h + a) % 2) * 4 + at_y) * 2 + (c + dc) % 2
        for half in (l, 1 - l)
        for a in (1, 0)
        for dc in (1, 0)
        for at_y in range(4)
    ]
    layer_keep, layer_send = call(
        reorder_kernel,
        "reorder",
        [jnp.stack(order).astype(jnp.int32), layer_input],
        [SMEM, VMEM],
        (shape(TOK, HALF),) * 2,
        (VMEM,) * 2,
        deps=[scaled_keep],
    )
    layer_pair = recv(layer_send, "l", 1)

    to_heads = call(
        pack_kernel,
        "pack",
        [queries, key_rows, value_rows, segment_ids],
        [VMEM] * 4,
        shape(8, TOK + 16, 768),
        VMEM,
        deps=[scaled_keep],
    )
    packed = lax.all_to_all(to_heads, SEQ, split_axis=0, concat_axis=0, tiled=True)
    scaled = scaled + ring(gate(scaled_pair, [packed] + scaled[1:]))

    attended, probs = call(
        forward_kernel,
        "attention_forward",
        [idx, packed],
        [SMEM, pl.BlockSpec((8, TOK + 16, 384), lambda i: (0, 0, i))],
        (shape(256, 1024), shape(2, 1024, 1024)),
        (
            pl.BlockSpec((HEAD, 1024), lambda i: (i, 0)),
            pl.BlockSpec((1, 1024, 1024), lambda i: (i, 0, 0)),
        ),
        grid=(2,),
    )
    attended_pair = recv(attended, "l", 1)
    layer = call(
        pair_kernel,
        "pair",
        [layer_keep, layer_pair],
        [VMEM, VMEM],
        shape(2 * TOK, HALF),
        VMEM,
        deps=[attended_pair, out_rows] + scaled[5:],
    )
    slab = lax.all_gather(layer, "x", axis=0, tiled=True)
    dout_keep, dout_send = call(
        dout_kernel,
        "dout",
        scaled + [out_rows, place],
        [VMEM] * 9 + [SMEM],
        (shape(1024, 256, dtype=F32), shape(1024, 256)),
        (VMEM, VMEM),
        deps=[layer],
    )
    dout = (dout_keep + recv(dout_send, "l", 1).astype(F32)).astype(BF16)

    out_send, out_keep = call(
        out_terms_kernel,
        "out_terms",
        scaled + [attended, attended_pair, place],
        [VMEM] * 10 + [SMEM],
        (shape(4, 2, 512, 128), shape(4, 2, 512, 128)),
        (VMEM, VMEM),
        deps=[dout_send],
    )
    terms_t = call(
        backward_kernel,
        "attention_backward",
        [idx, packed, probs, dout],
        [
            SMEM,
            pl.BlockSpec((8, TOK + 16, 384), lambda i: (0, 0, i)),
            pl.BlockSpec((1, 1024, 1024), lambda i: (i, 0, 0)),
            pl.BlockSpec((1024, HEAD), lambda i: (0, i)),
        ],
        shape(768, 1024),
        pl.BlockSpec((384, 1024), lambda i: (i, 0)),
        deps=[out_keep],
        grid=(2,),
        scratch=[pltpu.VMEM((HEAD, 1024), F32), pltpu.VMEM((HEAD, 1024), F32)],
    )
    terms_pair = recv(terms_t, "l", 1)

    def core_sum(send, keep):
        return add_low(keep, recv(send, "c", 1))

    def y_sum(blocks):
        arrived = lax.all_to_all(blocks, "y", split_axis=0, concat_axis=0, tiled=True)
        return jnp.sum(arrived.astype(F32), axis=0).astype(BF16)

    def y_permuted(blocks):
        part = 0.0
        for dy in (2, 1, 3, 0):
            block = lax.dynamic_index_in_dim(blocks, (y + dy) % 4, 0, keepdims=False)
            part = part + (recv(block, "y", 4 - dy) if dy else block).astype(F32)
        return part.astype(BF16)

    out_part = y_permuted(core_sum(gate(out_send, [terms_t]), out_keep))

    send, keep = term_blocks(terms_t, slab, place, False, [out_part])
    part = y_permuted(core_sum(send, keep))
    full = []
    for i, a in enumerate((1, 0)):
        for s in range(2):
            full.append(send_zz(part[i], lambda h1, h0, l: (l, h0 ^ a, l), s))

    grad_out = 0.0
    for a in range(2):
        for b in range(2):
            chosen = lax.dynamic_slice_in_dim(out_part[a], (h // 2 + b + l) % 2 * 256, 256, 0)
            chosen = send_zz(chosen, lambda h1, h0, l: (l, h0 ^ a, h1 ^ b))
            grad_out = grad_out + chosen.astype(F32)

    blocks = gate(core_sum(*term_blocks(terms_pair, slab, place, True, [keep])), [part])
    part = gate(y_sum(blocks), [grad_out] + full)
    for i, a in enumerate((1, 0)):
        for s in range(2):
            full.append(send_zz(part[i], lambda h1, h0, l: (l, h0 ^ a, 1 - l), s))
    grad_q, grad_k, grad_v = call(
        finish_kernel,
        "finish",
        full,
        [VMEM] * 8,
        tuple(shape(128, 256, dtype=F32) for _ in range(3)),
        (VMEM,) * 3,
    )
    return grad_q, grad_k, grad_v, grad_out


def solution(mesh):
    view = Mesh(mesh.devices.reshape(SIZES), AXES)
    tokens = P(DP + SEQ, None)
    return jax.shard_map(
        shards,
        mesh=view,
        in_specs=(
            tokens,
            tokens,
            tokens,
            tokens,
            tokens,
            P(SEQ, DP),
            P(DP, SEQ),
            P(DP),
            P(DP + SEQ),
        ),
        out_specs=(P(DP, SEQ), P(DP, SEQ), P(DP, SEQ), P(SEQ, DP)),
        check_vma=False,
    )
```

```python
import jax
import jax.numpy as jnp
from jax import lax
from jax.experimental import pallas as pl
from jax.experimental.pallas import tpu as pltpu
from jax.sharding import Mesh, PartitionSpec as P

HEAD = 128
TSTEPS = 1000
TOK = 128
AXES = ("h", "y", "c", "l", "x")
SIZES = (4, 4, 2, 2, 4)
DP = ("h", "y", "c")
SEQ = ("l", "x")
RELATIVE = [(dl, dx) for dl in range(2) for dx in range(4)]
HALF = 2048
F32, BF16 = jnp.float32, jnp.bfloat16
VMEM = pl.BlockSpec(memory_space=pltpu.VMEM)
SMEM = pl.BlockSpec(memory_space=pltpu.SMEM)
HBM = pl.BlockSpec(memory_space=pltpu.HBM)


def recv(block, axis, offset):
    n = SIZES[AXES.index(axis)]
    return lax.ppermute(block, axis, [((i + offset) % n, i) for i in range(n)])


def send_zz(block, target, only=None):
    pairs = []
    for h in range(4):
        for l in range(2):
            if only is None or only == h // 2:
                h1, h0, to_l = target(h // 2, h % 2, l)
                pairs.append((h * 2 + l, (h1 * 2 + h0) * 2 + to_l))
    return lax.ppermute(block, ("h", "l"), pairs)


def ring(block):
    near, far, across = recv(block, "x", 1), recv(block, "x", 3), recv(block, "x", 2)
    return [block, near, across, far]


def dot(a, b, dims):
    return lax.dot_general(a, b, (dims, ((), ())), preferred_element_type=F32)


def call(kernel, name, inputs, specs, out_shape, out_specs, deps=(), grid=(1,), scratch=()):
    n, m = len(inputs), len(deps)

    def body(*refs):
        kernel(*refs[:n], *refs[n + m :])

    def whole(spec, array):
        zeros = (0,) * len(array.shape)
        return pl.BlockSpec(array.shape, lambda i: zeros) if spec is VMEM else spec

    outs = out_shape if isinstance(out_shape, tuple) else (out_shape,)
    out_specs = out_specs if isinstance(out_specs, tuple) else (out_specs,)
    results = pl.pallas_call(
        body,
        grid=grid,
        out_shape=outs,
        in_specs=[whole(s, a) for s, a in zip(specs, inputs)] + [HBM] * m,
        out_specs=tuple(whole(s, a) for s, a in zip(out_specs, outs)),
        scratch_shapes=scratch,
        compiler_params=pltpu.CompilerParams(vmem_limit_bytes=60 * 2**20),
        cost_estimate=pl.CostEstimate(flops=0, bytes_accessed=0, transcendentals=0),
        name=name,
    )(*inputs, *deps)
    return results if isinstance(out_shape, tuple) else results[0]


def gate(x, deps):
    return pl.pallas_call(
        lambda *refs: None,
        out_shape=jax.ShapeDtypeStruct(x.shape, x.dtype),
        in_specs=[HBM] * (1 + len(deps)),
        out_specs=HBM,
        input_output_aliases={0: 0},
        cost_estimate=pl.CostEstimate(flops=0, bytes_accessed=0, transcendentals=0),
        name="gate",
    )(x, *deps)


def shape(*dims, dtype=BF16):
    return jax.ShapeDtypeStruct(dims, dtype)


def scale_kernel(place_ref, g_ref, w_ref, keep_ref, send_ref):
    w = w_ref[...]
    mine = pl.multiple_of(place_ref[3] * HALF, HALF)
    other = pl.multiple_of((1 - place_ref[3]) * HALF, HALF)
    keep_ref[...] = (g_ref[:, pl.ds(mine, HALF)].astype(F32) * w).astype(BF16)
    send_ref[...] = (g_ref[:, pl.ds(other, HALF)].astype(F32) * w).astype(BF16)


def pack_kernel(q_ref, k_ref, v_ref, s_ref, o_ref):
    segs = jnp.broadcast_to(s_ref[...].astype(F32), (16, TOK)).astype(BF16)
    for dest in range(8):
        for head in range(2):
            cols = slice((dest * 2 + head) * HEAD, (dest * 2 + head + 1) * HEAD)
            for j, ref in enumerate((q_ref, k_ref, v_ref)):
                at = slice((head * 3 + j) * HEAD, (head * 3 + j + 1) * HEAD)
                o_ref[dest, :TOK, at] = ref[:, cols]
                o_ref[dest, TOK:, at] = segs


def reorder_kernel(order_ref, x_ref, *o_refs):
    for i, ref in enumerate(o_refs):
        for j in range(16):
            start = pl.multiple_of(order_ref[i * 16 + j] * 128, 128)
            ref[:, j * 128 : (j + 1) * 128] = x_ref[:, pl.ds(start, 128)]


def pair_kernel(a_ref, b_ref, o_ref):
    o_ref[:TOK] = a_ref[...]
    o_ref[TOK:] = b_ref[...]


def load_rows(x_ref, idx_ref, part):
    cols = slice(part * HEAD, (part + 1) * HEAD)
    return jnp.concatenate([x_ref[idx_ref[r], :TOK, cols] for r in range(8)], axis=0)


def forward_kernel(idx_ref, x_ref, att_ref, p_ref):
    factor = HEAD ** (-0.5)
    keys = load_rows(x_ref, idx_ref, 1)
    values = load_rows(x_ref, idx_ref, 2)
    segs = [x_ref[idx_ref[r], TOK : TOK + 16, :HEAD].astype(F32)[:1] for r in range(8)]
    seg_row = jnp.concatenate(segs, axis=1)
    for blk in range(8):
        rows = slice(blk * TOK, (blk + 1) * TOK)
        q = x_ref[idx_ref[blk], :TOK, :HEAD]
        seg_col = jnp.broadcast_to(segs[blk], (TOK, TOK)).T[:, :1]
        scores = dot(q, keys, ((1,), (1,))) * factor
        scores = jnp.where(seg_col == seg_row, scores, -jnp.inf)
        shifted = jnp.exp(scores - jnp.max(scores, axis=-1, keepdims=True))
        probs = shifted * (1.0 / jnp.sum(shifted, axis=-1, keepdims=True))
        low = probs.astype(BF16)
        p_ref[0, rows, :] = low
        att_ref[:, rows] = dot(low, values, ((1,), (0,))).T.astype(BF16)


def backward_kernel(idx_ref, x_ref, p_ref, dout_ref, o_ref, dk_ref, dv_ref):
    factor = HEAD ** (-0.5)
    keys = load_rows(x_ref, idx_ref, 1)
    values = load_rows(x_ref, idx_ref, 2)
    for blk in range(4):
        rows = slice(blk * 256, (blk + 1) * 256)
        q = jnp.concatenate([x_ref[idx_ref[2 * blk + j], :TOK, :HEAD] for j in range(2)], axis=0)
        low = p_ref[0, rows, :]
        dout = dout_ref[rows, :]
        dprobs = dot(dout, values, ((1,), (1,)))
        probs = low.astype(F32)
        delta = jnp.sum(probs * dprobs, axis=-1, keepdims=True)
        dscores = (probs * (dprobs - delta) * factor).astype(BF16)
        o_ref[:HEAD, rows] = dot(dscores, keys, ((1,), (0,))).T.astype(BF16)
        dk = dot(q, dscores, ((0,), (0,)))
        dv = dot(dout, low, ((0,), (0,)))
        if blk == 0:
            dk_ref[...] = dk
            dv_ref[...] = dv
        else:
            dk_ref[...] += dk
            dv_ref[...] += dv
    o_ref[HEAD : 2 * HEAD, :] = dk_ref[...].astype(BF16)
    o_ref[2 * HEAD :, :] = dv_ref[...].astype(BF16)


def flipped(lhs):
    return jnp.concatenate([lhs[:, 512:], lhs[:, :512]], axis=1)


def by_x(lhs_ref, x, flip):
    blocks = []
    for at_x in range(4):
        for dl in range(2):
            row = (1 - dl if flip else dl) * 4 + (at_x - x + 4) % 4
            blocks.append(lhs_ref[:, pl.ds(pl.multiple_of(row * TOK, TOK), TOK)])
    return jnp.concatenate(blocks, axis=1)


def dout_kernel(*refs):
    pieces, (w_ref, place_ref, keep_ref, send_ref) = refs[:8], refs[8:]
    mine = pl.multiple_of(place_ref[3] * HALF, HALF)
    other = pl.multiple_of((1 - place_ref[3]) * HALF, HALF)
    for quarter in range(4):
        left = jnp.concatenate([p[...] for p in pieces[2 * quarter : 2 * quarter + 2]], axis=0)
        rows = slice(quarter * 256, (quarter + 1) * 256)
        keep_ref[rows, :] = dot(left, w_ref[:, pl.ds(mine, HALF)], ((1,), (1,)))
        at = (quarter + 2) % 4 * 256
        total = dot(left, w_ref[:, pl.ds(other, HALF)], ((1,), (1,)))
        send_ref[at : at + 256, :] = total.astype(BF16)


def out_terms_kernel(*refs):
    pieces, (own_ref, other_ref, place_ref, send_ref, keep_ref) = refs[:8], refs[8:]
    h0, c = place_ref[0] % 2, place_ref[2]
    att = jnp.concatenate([own_ref[...], flipped(other_ref[...])], axis=0)
    for tile in range(8):
        cols = slice(tile * 256, (tile + 1) * 256)
        rhs = jnp.concatenate([p[:, cols] for p in pieces], axis=0)
        term = dot(att, rhs, ((1,), (0,))).astype(BF16)
        at = tile % 4
        a = (tile // 4 + h0) % 2
        send_ref[at, a] = jnp.where(c == 0, term[:, 128:], term[:, :128])
        keep_ref[at, a] = jnp.where(c == 0, term[:, :128], term[:, 128:])


def term_blocks(lhs, slab, place, flip, deps):
    m = lhs.shape[0]

    def kernel(lhs_ref, slab_ref, place_ref, send_ref, keep_ref):
        left = by_x(lhs_ref, place_ref[4], flip)
        for tile in range(8):
            cols = slice(tile * 256, (tile + 1) * 256)
            term = dot(left, slab_ref[:, cols], ((1,), (0,))).astype(BF16)
            out = send_ref if tile % 4 < 2 else keep_ref
            out[tile % 2 * 2, tile // 4] = term[:, :128]
            out[tile % 2 * 2 + 1, tile // 4] = term[:, 128:]

    return call(
        kernel,
        "term_blocks",
        [lhs, slab, place],
        [VMEM, VMEM, SMEM],
        (shape(4, 2, m, 128), shape(4, 2, m, 128)),
        (VMEM, VMEM),
        deps=deps,
    )


def finish_kernel(*refs):
    parts, outs = refs[:8], refs[8:]
    for head in range(2):
        for j in range(3):
            rows = slice((head * 3 + j) * HEAD, (head * 3 + j + 1) * HEAD)
            total = sum(r[rows, :].astype(F32) for r in parts)
            outs[j][:, head * HEAD : (head + 1) * HEAD] = total.T
    outs[3][...] = sum(r[768:, :].astype(F32) for r in parts)


def add_low(a, b):
    return (a.astype(F32) + b.astype(F32)).astype(BF16)


def shards(
    layer_input,
    queries,
    key_rows,
    value_rows,
    output_grad,
    out_weight,
    segment_ids,
    timesteps,
    masked_tokens,
):
    total_tokens = layer_input.shape[0] * 256
    norm_scale = float(total_tokens) ** (-0.5)
    h, y, c, l, x = (lax.axis_index(a) for a in AXES)
    idx = jnp.stack([((l + dl) % 2) * 4 + (x + dx) % 4 for dl, dx in RELATIVE]).astype(jnp.int32)
    place = jnp.stack([h, y, c, l, x]).astype(jnp.int32)

    out_rows = send_zz(out_weight, lambda h1, h0, to_l: (to_l, h0, h1))
    out_rows = lax.all_gather(out_rows, DP, axis=1, tiled=True)

    row_weight = masked_tokens.astype(F32) * (TSTEPS / timesteps.astype(F32)) * norm_scale
    scaled_keep, scaled_send = call(
        scale_kernel,
        "scale",
        [place, output_grad, row_weight[:, None]],
        [SMEM, VMEM, VMEM],
        (shape(TOK, HALF), shape(TOK, HALF)),
        (VMEM, VMEM),
    )
    scaled_pair = recv(scaled_send, "l", 1)
    scaled = ring(scaled_keep)
    order = [
        ((half * 2 + (h + a) % 2) * 4 + at_y) * 2 + (c + dc) % 2
        for half in (l, 1 - l)
        for a in (1, 0)
        for dc in (1, 0)
        for at_y in range(4)
    ]
    layer_keep, layer_send = call(
        reorder_kernel,
        "reorder",
        [jnp.stack(order).astype(jnp.int32), layer_input],
        [SMEM, VMEM],
        (shape(TOK, HALF),) * 2,
        (VMEM,) * 2,
        deps=[scaled_keep],
    )
    layer_pair = recv(layer_send, "l", 1)

    to_heads = call(
        pack_kernel,
        "pack",
        [queries, key_rows, value_rows, segment_ids],
        [VMEM] * 4,
        shape(8, TOK + 16, 768),
        VMEM,
        deps=[scaled_keep],
    )
    packed = lax.all_to_all(to_heads, SEQ, split_axis=0, concat_axis=0, tiled=True)
    scaled = scaled + ring(gate(scaled_pair, [packed] + scaled[1:]))

    attended, probs = call(
        forward_kernel,
        "attention_forward",
        [idx, packed],
        [SMEM, pl.BlockSpec((8, TOK + 16, 384), lambda i: (0, 0, i))],
        (shape(256, 1024), shape(2, 1024, 1024)),
        (
            pl.BlockSpec((HEAD, 1024), lambda i: (i, 0)),
            pl.BlockSpec((1, 1024, 1024), lambda i: (i, 0, 0)),
        ),
        grid=(2,),
    )
    attended_pair = recv(attended, "l", 1)
    layer = call(
        pair_kernel,
        "pair",
        [layer_keep, layer_pair],
        [VMEM, VMEM],
        shape(2 * TOK, HALF),
        VMEM,
        deps=[attended_pair, out_rows] + scaled[5:],
    )
    slab = lax.all_gather(layer, "x", axis=0, tiled=True)
    dout_keep, dout_send = call(
        dout_kernel,
        "dout",
        scaled + [out_rows, place],
        [VMEM] * 9 + [SMEM],
        (shape(1024, 256, dtype=F32), shape(1024, 256)),
        (VMEM, VMEM),
        deps=[layer],
    )
    dout = (dout_keep + recv(dout_send, "l", 1).astype(F32)).astype(BF16)

    out_send, out_keep = call(
        out_terms_kernel,
        "out_terms",
        scaled + [attended, attended_pair, place],
        [VMEM] * 10 + [SMEM],
        (shape(4, 2, 512, 128), shape(4, 2, 512, 128)),
        (VMEM, VMEM),
        deps=[dout_send],
    )
    terms_t = call(
        backward_kernel,
        "attention_backward",
        [idx, packed, probs, dout],
        [
            SMEM,
            pl.BlockSpec((8, TOK + 16, 384), lambda i: (0, 0, i)),
            pl.BlockSpec((1, 1024, 1024), lambda i: (i, 0, 0)),
            pl.BlockSpec((1024, HEAD), lambda i: (0, i)),
        ],
        shape(768, 1024),
        pl.BlockSpec((384, 1024), lambda i: (i, 0)),
        deps=[out_keep],
        grid=(2,),
        scratch=[pltpu.VMEM((HEAD, 1024), F32), pltpu.VMEM((HEAD, 1024), F32)],
    )
    terms_pair = recv(terms_t, "l", 1)

    def core_sum(send, keep):
        return add_low(keep, recv(send, "c", 1))

    def y_permuted(blocks):
        part = 0.0
        for dy in (2, 1, 3, 0):
            block = lax.dynamic_index_in_dim(blocks, (y + dy) % 4, 0, keepdims=False)
            part = part + (recv(block, "y", 4 - dy) if dy else block).astype(F32)
        return part

    out_part = y_permuted(core_sum(gate(out_send, [terms_t]), out_keep)).astype(BF16)

    send, keep = term_blocks(terms_t, slab, place, False, [out_part])
    part = y_permuted(core_sum(send, keep))
    full, own_sums = [], []
    for i, a in enumerate((1, 0)):
        both = jnp.concatenate([part[i].astype(BF16), out_part[a, :256]], axis=0)
        own_sums.append(both)
        for s in range(2):
            full.append(send_zz(both, lambda h1, h0, l: (l, h0 ^ a, l), s))
    own = full[:]
    blocks = gate(core_sum(*term_blocks(terms_pair, slab, place, True, [keep])), own_sums)
    arrived = lax.all_to_all(blocks, "y", split_axis=0, concat_axis=0, tiled=True)
    for i, a in enumerate((1, 0)):
        total = jnp.sum(arrived[:, i].astype(F32), axis=0).astype(BF16)
        both = gate(jnp.concatenate([total, out_part[a, 256:]], axis=0), own[2 * i : 2 * i + 2])
        for s in range(2):
            full.append(send_zz(both, lambda h1, h0, l: (l, h0 ^ a, 1 - l), s))
    return call(
        finish_kernel,
        "finish",
        full,
        [VMEM] * 8,
        tuple(shape(128, 256, dtype=F32) for _ in range(3)) + (shape(256, 128, dtype=F32),),
        (VMEM,) * 4,
    )


def solution(mesh):
    view = Mesh(mesh.devices.reshape(SIZES), AXES)
    tokens = P(DP + SEQ, None)
    return jax.shard_map(
        shards,
        mesh=view,
        in_specs=(
            tokens,
            tokens,
            tokens,
            tokens,
            tokens,
            P(SEQ, DP),
            P(DP, SEQ),
            P(DP),
            P(DP + SEQ),
        ),
        out_specs=(P(DP, SEQ), P(DP, SEQ), P(DP, SEQ), P(SEQ, DP)),
        check_vma=False,
    )
```

```python
import jax
import jax.numpy as jnp
from jax import lax
from jax.experimental import pallas as pl
from jax.experimental.pallas import tpu as pltpu
from jax.sharding import Mesh, PartitionSpec as P

HEAD = 128
TSTEPS = 1000
TOK = 128
AXES = ("h", "y", "c", "l", "x")
SIZES = (4, 4, 2, 2, 4)
DP = ("h", "y", "c")
SEQ = ("l", "x")
RELATIVE = [(dl, dx) for dl in range(2) for dx in range(4)]
HALF = 2048
F32, BF16 = jnp.float32, jnp.bfloat16
VMEM = pl.BlockSpec(memory_space=pltpu.VMEM)
SMEM = pl.BlockSpec(memory_space=pltpu.SMEM)
HBM = pl.BlockSpec(memory_space=pltpu.HBM)


def recv(block, axis, offset):
    n = SIZES[AXES.index(axis)]
    return lax.ppermute(block, axis, [((i + offset) % n, i) for i in range(n)])


def send_zz(block, target, only=None):
    pairs = []
    for h in range(4):
        for l in range(2):
            if only is None or only == h // 2:
                h1, h0, to_l = target(h // 2, h % 2, l)
                pairs.append((h * 2 + l, (h1 * 2 + h0) * 2 + to_l))
    return lax.ppermute(block, ("h", "l"), pairs)


def ring(block):
    near, far, across = recv(block, "x", 1), recv(block, "x", 3), recv(block, "x", 2)
    return [block, near, across, far]


def dot(a, b, dims):
    return lax.dot_general(a, b, (dims, ((), ())), preferred_element_type=F32)


def call(kernel, name, inputs, specs, out_shape, out_specs, deps=(), grid=(1,), scratch=()):
    n, m = len(inputs), len(deps)

    def body(*refs):
        kernel(*refs[:n], *refs[n + m :])

    def whole(spec, array):
        zeros = (0,) * len(array.shape)
        return pl.BlockSpec(array.shape, lambda i: zeros) if spec is VMEM else spec

    outs = out_shape if isinstance(out_shape, tuple) else (out_shape,)
    out_specs = out_specs if isinstance(out_specs, tuple) else (out_specs,)
    results = pl.pallas_call(
        body,
        grid=grid,
        out_shape=outs,
        in_specs=[whole(s, a) for s, a in zip(specs, inputs)] + [HBM] * m,
        out_specs=tuple(whole(s, a) for s, a in zip(out_specs, outs)),
        scratch_shapes=scratch,
        compiler_params=pltpu.CompilerParams(vmem_limit_bytes=60 * 2**20),
        cost_estimate=pl.CostEstimate(flops=0, bytes_accessed=0, transcendentals=0),
        name=name,
    )(*inputs, *deps)
    return results if isinstance(out_shape, tuple) else results[0]


def gate(x, deps):
    return pl.pallas_call(
        lambda *refs: None,
        out_shape=jax.ShapeDtypeStruct(x.shape, x.dtype),
        in_specs=[HBM] * (1 + len(deps)),
        out_specs=HBM,
        input_output_aliases={0: 0},
        cost_estimate=pl.CostEstimate(flops=0, bytes_accessed=0, transcendentals=0),
        name="gate",
    )(x, *deps)


def shape(*dims, dtype=BF16):
    return jax.ShapeDtypeStruct(dims, dtype)


def scale_kernel(place_ref, g_ref, w_ref, keep_ref, send_ref):
    w = w_ref[...]
    mine = pl.multiple_of(place_ref[3] * HALF, HALF)
    other = pl.multiple_of((1 - place_ref[3]) * HALF, HALF)
    keep_ref[...] = (g_ref[:, pl.ds(mine, HALF)].astype(F32) * w).astype(BF16)
    send_ref[...] = (g_ref[:, pl.ds(other, HALF)].astype(F32) * w).astype(BF16)


def pack_kernel(q_ref, k_ref, v_ref, s_ref, o_ref):
    segs = jnp.broadcast_to(s_ref[...].astype(F32), (16, TOK)).astype(BF16)
    for dest in range(8):
        for head in range(2):
            cols = slice((dest * 2 + head) * HEAD, (dest * 2 + head + 1) * HEAD)
            for j, ref in enumerate((q_ref, k_ref, v_ref)):
                at = slice((head * 3 + j) * HEAD, (head * 3 + j + 1) * HEAD)
                o_ref[dest, :TOK, at] = ref[:, cols]
                o_ref[dest, TOK:, at] = segs


def reorder_kernel(order_ref, x_ref, *o_refs):
    for i, ref in enumerate(o_refs):
        for j in range(16):
            start = pl.multiple_of(order_ref[i * 16 + j] * 128, 128)
            ref[:, j * 128 : (j + 1) * 128] = x_ref[:, pl.ds(start, 128)]


def pair_kernel(a_ref, b_ref, o_ref):
    o_ref[:TOK] = a_ref[...]
    o_ref[TOK:] = b_ref[...]


def load_rows(x_ref, idx_ref, part):
    cols = slice(part * HEAD, (part + 1) * HEAD)
    return jnp.concatenate([x_ref[idx_ref[r], :TOK, cols] for r in range(8)], axis=0)


def forward_kernel(idx_ref, x_ref, att_ref, p_ref):
    factor = HEAD ** (-0.5)
    keys = load_rows(x_ref, idx_ref, 1)
    values = load_rows(x_ref, idx_ref, 2)
    segs = [x_ref[idx_ref[r], TOK : TOK + 16, :HEAD].astype(F32)[:1] for r in range(8)]
    seg_row = jnp.concatenate(segs, axis=1)
    for blk in range(8):
        rows = slice(blk * TOK, (blk + 1) * TOK)
        q = x_ref[idx_ref[blk], :TOK, :HEAD]
        seg_col = jnp.broadcast_to(segs[blk], (TOK, TOK)).T[:, :1]
        scores = dot(q, keys, ((1,), (1,))) * factor
        scores = jnp.where(seg_col == seg_row, scores, -jnp.inf)
        shifted = jnp.exp(scores - jnp.max(scores, axis=-1, keepdims=True))
        probs = shifted * (1.0 / jnp.sum(shifted, axis=-1, keepdims=True))
        low = probs.astype(BF16)
        p_ref[0, rows, :] = low
        att_ref[:, rows] = dot(low, values, ((1,), (0,))).T.astype(BF16)


def backward_kernel(idx_ref, x_ref, p_ref, dout_ref, o_ref, dk_ref, dv_ref):
    factor = HEAD ** (-0.5)
    keys = load_rows(x_ref, idx_ref, 1)
    values = load_rows(x_ref, idx_ref, 2)
    for blk in range(4):
        rows = slice(blk * 256, (blk + 1) * 256)
        q = jnp.concatenate([x_ref[idx_ref[2 * blk + j], :TOK, :HEAD] for j in range(2)], axis=0)
        low = p_ref[0, rows, :]
        dout = dout_ref[rows, :]
        dprobs = dot(dout, values, ((1,), (1,)))
        probs = low.astype(F32)
        delta = jnp.sum(probs * dprobs, axis=-1, keepdims=True)
        dscores = (probs * (dprobs - delta) * factor).astype(BF16)
        o_ref[:HEAD, rows] = dot(dscores, keys, ((1,), (0,))).T.astype(BF16)
        dk = dot(q, dscores, ((0,), (0,)))
        dv = dot(dout, low, ((0,), (0,)))
        if blk == 0:
            dk_ref[...] = dk
            dv_ref[...] = dv
        else:
            dk_ref[...] += dk
            dv_ref[...] += dv
    o_ref[HEAD : 2 * HEAD, :] = dk_ref[...].astype(BF16)
    o_ref[2 * HEAD :, :] = dv_ref[...].astype(BF16)


def flipped(lhs):
    return jnp.concatenate([lhs[:, 512:], lhs[:, :512]], axis=1)


def by_x(lhs_ref, x, flip):
    blocks = []
    for at_x in range(4):
        for dl in range(2):
            row = (1 - dl if flip else dl) * 4 + (at_x - x + 4) % 4
            blocks.append(lhs_ref[:, pl.ds(pl.multiple_of(row * TOK, TOK), TOK)])
    return jnp.concatenate(blocks, axis=1)


def dout_kernel(*refs):
    pieces, (w_ref, place_ref, keep_ref, send_ref) = refs[:8], refs[8:]
    mine = pl.multiple_of(place_ref[3] * HALF, HALF)
    other = pl.multiple_of((1 - place_ref[3]) * HALF, HALF)
    for quarter in range(4):
        left = jnp.concatenate([p[...] for p in pieces[2 * quarter : 2 * quarter + 2]], axis=0)
        rows = slice(quarter * 256, (quarter + 1) * 256)
        keep_ref[rows, :] = dot(left, w_ref[:, pl.ds(mine, HALF)], ((1,), (1,)))
        at = (quarter + 2) % 4 * 256
        total = dot(left, w_ref[:, pl.ds(other, HALF)], ((1,), (1,)))
        send_ref[at : at + 256, :] = total.astype(BF16)


def out_terms_kernel(*refs):
    pieces, (own_ref, other_ref, place_ref, send_ref, keep_ref) = refs[:8], refs[8:]
    h0, c = place_ref[0] % 2, place_ref[2]
    att = jnp.concatenate([own_ref[...], flipped(other_ref[...])], axis=0)
    for tile in range(8):
        cols = slice(tile * 256, (tile + 1) * 256)
        rhs = jnp.concatenate([p[:, cols] for p in pieces], axis=0)
        term = dot(att, rhs, ((1,), (0,))).astype(BF16)
        at = tile % 4
        a = (tile // 4 + h0) % 2
        send_ref[at, a] = jnp.where(c == 0, term[:, 128:], term[:, :128])
        keep_ref[at, a] = jnp.where(c == 0, term[:, :128], term[:, 128:])


def term_blocks(lhs, slab, place, flip, deps):
    m = lhs.shape[0]

    def kernel(lhs_ref, slab_ref, place_ref, send_ref, keep_ref):
        left = by_x(lhs_ref, place_ref[4], flip)
        for tile in range(8):
            cols = slice(tile * 256, (tile + 1) * 256)
            term = dot(left, slab_ref[:, cols], ((1,), (0,))).astype(BF16)
            out = send_ref if tile % 4 < 2 else keep_ref
            out[tile % 2 * 2, tile // 4] = term[:, :128]
            out[tile % 2 * 2 + 1, tile // 4] = term[:, 128:]

    return call(
        kernel,
        "term_blocks",
        [lhs, slab, place],
        [VMEM, VMEM, SMEM],
        (shape(4, 2, m, 128), shape(4, 2, m, 128)),
        (VMEM, VMEM),
        deps=deps,
    )


def finish_kernel(*refs):
    parts, outs = refs[:8], refs[8:]
    for head in range(2):
        for j in range(3):
            rows = slice((head * 3 + j) * HEAD, (head * 3 + j + 1) * HEAD)
            total = sum(r[rows, :].astype(F32) for r in parts)
            outs[j][:, head * HEAD : (head + 1) * HEAD] = total.T
    outs[3][...] = sum(r[768:, :].astype(F32) for r in parts)


def add_low(a, b):
    return (a.astype(F32) + b.astype(F32)).astype(BF16)


def shards(
    layer_input,
    queries,
    key_rows,
    value_rows,
    output_grad,
    out_weight,
    segment_ids,
    timesteps,
    masked_tokens,
):
    total_tokens = layer_input.shape[0] * 256
    norm_scale = float(total_tokens) ** (-0.5)
    h, y, c, l, x = (lax.axis_index(a) for a in AXES)
    idx = jnp.stack([((l + dl) % 2) * 4 + (x + dx) % 4 for dl, dx in RELATIVE]).astype(jnp.int32)
    place = jnp.stack([h, y, c, l, x]).astype(jnp.int32)

    out_rows = send_zz(out_weight, lambda h1, h0, to_l: (to_l, h0, h1))
    out_rows = lax.all_gather(out_rows, DP, axis=1, tiled=True)

    row_weight = masked_tokens.astype(F32) * (TSTEPS / timesteps.astype(F32)) * norm_scale
    scaled_keep, scaled_send = call(
        scale_kernel,
        "scale",
        [place, output_grad, row_weight[:, None]],
        [SMEM, VMEM, VMEM],
        (shape(TOK, HALF), shape(TOK, HALF)),
        (VMEM, VMEM),
    )
    scaled_pair = recv(scaled_send, "l", 1)
    scaled = ring(scaled_keep)

    to_heads = call(
        pack_kernel,
        "pack",
        [queries, key_rows, value_rows, segment_ids],
        [VMEM] * 4,
        shape(8, TOK + 16, 768),
        VMEM,
        deps=[scaled_keep],
    )
    packed = lax.all_to_all(to_heads, SEQ, split_axis=0, concat_axis=0, tiled=True)
    order = [
        ((half * 2 + (h + a) % 2) * 4 + at_y) * 2 + (c + dc) % 2
        for half in (l, 1 - l)
        for a in (1, 0)
        for dc in (1, 0)
        for at_y in range(4)
    ]
    layer_keep, layer_send = call(
        reorder_kernel,
        "reorder",
        [jnp.stack(order).astype(jnp.int32), layer_input],
        [SMEM, VMEM],
        (shape(TOK, HALF),) * 2,
        (VMEM,) * 2,
        deps=[packed],
    )
    layer_pair = recv(layer_send, "l", 1)
    scaled = scaled + ring(gate(scaled_pair, [packed] + scaled[1:]))

    attended, probs = call(
        forward_kernel,
        "attention_forward",
        [idx, packed],
        [SMEM, pl.BlockSpec((8, TOK + 16, 384), lambda i: (0, 0, i))],
        (shape(256, 1024), shape(2, 1024, 1024)),
        (
            pl.BlockSpec((HEAD, 1024), lambda i: (i, 0)),
            pl.BlockSpec((1, 1024, 1024), lambda i: (i, 0, 0)),
        ),
        grid=(2,),
    )
    attended_pair = recv(attended, "l", 1)
    layer = call(
        pair_kernel,
        "pair",
        [layer_keep, layer_pair],
        [VMEM, VMEM],
        shape(2 * TOK, HALF),
        VMEM,
        deps=[attended_pair, out_rows] + scaled[5:],
    )
    slab = lax.all_gather(layer, "x", axis=0, tiled=True)
    dout_keep, dout_send = call(
        dout_kernel,
        "dout",
        scaled + [out_rows, place],
        [VMEM] * 9 + [SMEM],
        (shape(1024, 256, dtype=F32), shape(1024, 256)),
        (VMEM, VMEM),
        deps=[layer],
    )
    dout = (dout_keep + recv(dout_send, "l", 1).astype(F32)).astype(BF16)

    out_send, out_keep = call(
        out_terms_kernel,
        "out_terms",
        scaled + [attended, attended_pair, place],
        [VMEM] * 10 + [SMEM],
        (shape(4, 2, 512, 128), shape(4, 2, 512, 128)),
        (VMEM, VMEM),
        deps=[dout_send],
    )
    terms_t = call(
        backward_kernel,
        "attention_backward",
        [idx, packed, probs, dout],
        [
            SMEM,
            pl.BlockSpec((8, TOK + 16, 384), lambda i: (0, 0, i)),
            pl.BlockSpec((1, 1024, 1024), lambda i: (i, 0, 0)),
            pl.BlockSpec((1024, HEAD), lambda i: (0, i)),
        ],
        shape(768, 1024),
        pl.BlockSpec((384, 1024), lambda i: (i, 0)),
        deps=[out_keep],
        grid=(2,),
        scratch=[pltpu.VMEM((HEAD, 1024), F32), pltpu.VMEM((HEAD, 1024), F32)],
    )
    terms_pair = recv(terms_t, "l", 1)

    def core_sum(send, keep):
        return add_low(keep, recv(send, "c", 1))

    def y_permuted(blocks):
        part = 0.0
        for dy in (2, 1, 3, 0):
            block = lax.dynamic_index_in_dim(blocks, (y + dy) % 4, 0, keepdims=False)
            part = part + (recv(block, "y", 4 - dy) if dy else block).astype(F32)
        return part

    out_part = y_permuted(core_sum(gate(out_send, [terms_t]), out_keep)).astype(BF16)

    send, keep = term_blocks(terms_t, slab, place, False, [out_part])
    part = y_permuted(core_sum(send, keep))
    full, own_sums = [], []
    for i, a in enumerate((1, 0)):
        both = jnp.concatenate([part[i].astype(BF16), out_part[a, :256]], axis=0)
        own_sums.append(both)
        for s in range(2):
            full.append(send_zz(both, lambda h1, h0, l: (l, h0 ^ a, l), s))
    own = full[:]
    blocks = gate(core_sum(*term_blocks(terms_pair, slab, place, True, [keep])), own_sums)
    arrived = lax.all_to_all(blocks, "y", split_axis=0, concat_axis=0, tiled=True)
    for i, a in enumerate((1, 0)):
        total = jnp.sum(arrived[:, i].astype(F32), axis=0).astype(BF16)
        both = gate(jnp.concatenate([total, out_part[a, 256:]], axis=0), own[2 * i : 2 * i + 2])
        for s in range(2):
            full.append(send_zz(both, lambda h1, h0, l: (l, h0 ^ a, 1 - l), s))
    return call(
        finish_kernel,
        "finish",
        full,
        [VMEM] * 8,
        tuple(shape(128, 256, dtype=F32) for _ in range(3)) + (shape(256, 128, dtype=F32),),
        (VMEM,) * 4,
    )


def solution(mesh):
    view = Mesh(mesh.devices.reshape(SIZES), AXES)
    tokens = P(DP + SEQ, None)
    return jax.shard_map(
        shards,
        mesh=view,
        in_specs=(
            tokens,
            tokens,
            tokens,
            tokens,
            tokens,
            P(SEQ, DP),
            P(DP, SEQ),
            P(DP),
            P(DP + SEQ),
        ),
        out_specs=(P(DP, SEQ), P(DP, SEQ), P(DP, SEQ), P(SEQ, DP)),
        check_vma=False,
    )
```
